32 devices in a mesh: tm: 16 (over z, x, core), dish: 2 (over y).
Axes of the slice: x: 2, y: 2, z: 4, core: 2. Of those that a mesh axis runs over, the one named last changes fastest.
Arguments:
- voltages: bfloat16 [2, 64, 65536], P(None, 'dish', 'tm'), may hold values from -6 to 6
- beam_weights: bfloat16 [2, 64], P(None, 'dish'), may hold values from -0.75 to 0.75
- phase_bins: int32 [65536], P('tm'), may hold values from 0 to 1023, as said below
Outputs:
- spectrum: float32 [2048, 2, 1024], P('dish', None, 'tm')
The draws below stay inside these ranges and needn't reach their ends.
Inputs may be any that keep to these rules, and one draw needn't show every extreme that they name: `phase_bins`: from each time sample to the next the bin stays or advances by one, wrapping from 1023 to 0; every bin occurs.
All inputs are finite; a program needn't handle non-finite values.
Results may differ from the reference program's by a relative error of at most 0.0039.
Values may be sent and summed in bfloat16 or wider, within the bound.
A program may use at most 128 MiB of HBM per device.

```python
import math
import jax
import jax.numpy as jnp
from jax import lax

DISHES = 64
PH = 1024
LAGS = 2048
SAMPLES = 65536


def draw_phase_bins(key, part):
    tick_total = 1048576
    first_key, second_key = jax.random.split(jax.random.fold_in(key, 17))
    increments = jax.random.randint(first_key, (SAMPLES,), tick_total // (4 * PH), tick_total // PH)
    offset = jax.random.randint(second_key, (), 0, tick_total)
    phase_ticks = (offset + jnp.cumsum(increments)) % tick_total
    return (phase_ticks * PH // tick_total).astype(jnp.int32)


def steps_of(stream_key, extent, cuts, low, top_value):
    def one(position, shards_of):
        steps = jax.random.uniform(jax.random.fold_in(jax.random.fold_in(stream_key, 6), position), (shards_of,), jnp.float32, low / len(cuts), top_value / len(cuts))
        return jnp.repeat(jnp.exp(steps), extent[position] // shards_of).reshape((-1,) + (1,) * (len(extent) - position - 1))

    gain = one(*cuts[0])
    for cut in cuts[1:]:
        gain = gain * one(*cut)
    return gain


def bell_draw(key, shape, deviation, most, cuts=(), kind=jnp.bfloat16):
    drawn = jax.random.normal(key, shape, jnp.float32) * deviation
    if len(cuts) > 0:
        drawn = steps_of(key, shape, cuts, -0.22, 0.18) * drawn
    return jnp.clip(drawn, min=-most, max=most).astype(kind)


def setup_inputs(seed: int = 0) -> dict:
    arg_keys = jax.random.split(jax.random.key(seed), 4)
    voltages = bell_draw(arg_keys[0], (2, DISHES, SAMPLES), 1.0, 6.0, ((1, 2), (2, 16)))
    beam_weights = bell_draw(arg_keys[1], (2, DISHES), DISHES ** -0.5, 0.75, ((1, 2),))
    phase_bins = draw_phase_bins(jax.random.fold_in(arg_keys[3], 71), 0)
    return {"voltages": voltages, "beam_weights": beam_weights, "phase_bins": phase_bins}


def reference(voltages, beam_weights, phase_bins):
    real_beam = jnp.dot(beam_weights[0], voltages[0], preferred_element_type=jnp.float32) - jnp.dot(beam_weights[1], voltages[1], preferred_element_type=jnp.float32)
    imag_beam = jnp.dot(beam_weights[1], voltages[0], preferred_element_type=jnp.float32) + jnp.dot(beam_weights[0], voltages[1], preferred_element_type=jnp.float32)
    beam_pair = jnp.stack([real_beam, imag_beam]).astype(jnp.bfloat16)
    padded = jnp.pad(beam_pair.astype(jnp.float32), ((0, 0), (0, LAGS)))
    block_rows = min(512, SAMPLES)
    block_total = SAMPLES // block_rows
    lag_grid = jnp.arange(block_rows, dtype=jnp.int32)[:, None] + jnp.arange(LAGS, dtype=jnp.int32)[None, :]

    def fold_step(carry, block_index):
        row_start = (block_index * block_rows).astype(jnp.int32)
        segment = lax.dynamic_slice_in_dim(padded, row_start, block_rows + LAGS, 1)
        hankel = segment[:, lag_grid]
        current = segment[:, :block_rows]
        real_term = current[0][:, None] * hankel[0] + current[1][:, None] * hankel[1]
        imag_term = current[0][:, None] * hankel[1] - current[1][:, None] * hankel[0]
        bin_block = lax.dynamic_slice_in_dim(phase_bins, row_start, block_rows)
        real_sum = jax.ops.segment_sum(real_term, bin_block, PH)
        imag_sum = jax.ops.segment_sum(imag_term, bin_block, PH)
        return ((carry[0] + real_sum, carry[1] + imag_sum), None)
    zero_fold = jnp.zeros((PH, LAGS), jnp.float32)
    folds, unused = lax.scan(fold_step, (zero_fold, zero_fold), jnp.arange(block_total, dtype=jnp.int32))
    scale_factor = 1.0 / math.sqrt(LAGS * SAMPLES / PH)
    transformed = jnp.fft.fft(folds[0] + 1j * folds[1], axis=1) * scale_factor
    real_out = jnp.real(transformed).astype(jnp.float32)
    imag_out = jnp.imag(transformed).astype(jnp.float32)
    return jnp.stack([real_out.T, imag_out.T], 1)
```

```python
import functools
import math

import jax
import jax.numpy as jnp
import ml_dtypes
import numpy as np
from jax import lax
from jax.experimental import pallas as pl
from jax.experimental.pallas import tpu as pltpu
from jax.sharding import PartitionSpec as P

PH = 1024
LAGS = 2048
BLOCK = 128
GROUP = 16
LAG_PIECE = 512


def form_beam(volt_block, weights):
    dish_count = volt_block.shape[1]
    mixer_rows = jnp.stack(
        [jnp.concatenate([weights[0], -weights[1]]), jnp.concatenate([weights[1], weights[0]])]
    )
    flat_volts = volt_block.reshape(2 * dish_count, volt_block.shape[2])
    return jnp.dot(mixer_rows, flat_volts, preferred_element_type=jnp.float32)


def fold_kernel(chunk, bin_count, list_ref, count_ref, base_ref, beam_ref, bins_ref, out_ref, shifted, hankel):
    step = pl.program_id(0)
    start = pl.multiple_of(step * chunk, BLOCK)
    width = chunk + LAGS
    blocks_here = chunk // BLOCK

    @pl.when(step == 0)
    def _():
        out_ref[...] = jnp.zeros_like(out_ref)

    count = count_ref[step]

    @pl.when(count > 0)
    def _():
        row = lax.broadcasted_iota(jnp.int32, (GROUP, 2 * BLOCK), 0)

        def shift_rows(position, carry):
            lane = pl.multiple_of(position * BLOCK, BLOCK)
            for part in range(2):
                rows = jnp.broadcast_to(
                    beam_ref[pl.ds(part, 1), pl.ds(pl.multiple_of(start + lane, BLOCK), 2 * BLOCK)],
                    (GROUP, 2 * BLOCK),
                )
                amount = 1
                while amount < GROUP:
                    rows = jnp.where(
                        (row & amount) != 0, pltpu.roll(rows, 2 * BLOCK - amount, 1), rows
                    )
                    amount *= 2
                shifted[part, :, pl.ds(lane, BLOCK)] = rows[:, :BLOCK]
            return carry

        lax.fori_loop(0, width // BLOCK, shift_rows, 0)
        lane_index = lax.broadcasted_iota(jnp.int32, (GROUP, BLOCK), 1)

        def build(position, carry):
            lane = pl.multiple_of(position * BLOCK, BLOCK)
            for part in range(2):
                near = shifted[part, :, pl.ds(lane, BLOCK)]
                far = shifted[part, :, pl.ds(lane + BLOCK, BLOCK)]
                for group in range(BLOCK // GROUP):
                    offset = group * GROUP
                    if offset == 0:
                        piece = near
                    else:
                        mixed = jnp.where(lane_index < offset, far, near)
                        piece = pltpu.roll(mixed, BLOCK - offset, 1)
                    hankel[pl.ds(pl.multiple_of(lane + offset, GROUP), GROUP), pl.ds(part * BLOCK, BLOCK)] = (
                        piece.astype(jnp.bfloat16)
                    )
            return carry

        lax.fori_loop(0, width // BLOCK - 1, build, 0)
        target = base_ref[0] + lax.broadcasted_iota(jnp.int32, (bin_count, BLOCK), 0)

        def fold(position, carry):
            row_start = pl.multiple_of(list_ref[step * blocks_here + position] * BLOCK, BLOCK)
            lane = pl.ds(pl.multiple_of(start + row_start, BLOCK), BLOCK)
            real = beam_ref[0:1, lane]
            imag = beam_ref[1:2, lane]
            chosen = bins_ref[0:1, lane] == target
            zero = jnp.zeros((bin_count, BLOCK), jnp.float32)
            chosen_real = jnp.where(chosen, real, zero)
            chosen_imag = jnp.where(chosen, imag, zero)
            right = jnp.concatenate(
                [
                    jnp.concatenate([chosen_real, chosen_imag], 1),
                    jnp.concatenate([-chosen_imag, chosen_real], 1),
                ],
                0,
            ).astype(jnp.bfloat16)
            for piece in range(LAGS // LAG_PIECE):
                rows = pl.ds(piece * LAG_PIECE, LAG_PIECE)
                left = hankel[pl.ds(pl.multiple_of(row_start + piece * LAG_PIECE, BLOCK), LAG_PIECE), :]
                out_ref[rows, :] += lax.dot_general(
                    left, right, (((1,), (1,)), ((), ())), preferred_element_type=jnp.float32
                )
            return carry

        lax.fori_loop(0, count, fold, 0)


def transform_table(row_count):
    turn = np.arange(row_count)[:, None] * np.arange(LAGS)[None, :] % LAGS
    angle = turn * (2.0 * math.pi / LAGS)
    return np.concatenate([np.cos(angle), np.sin(angle)], 0).astype(ml_dtypes.bfloat16)


def per_device(table, voltages, beam_weights, phase_bins):
    samples = phase_bins.shape[0]
    count_tm = lax.axis_size("tm")
    count_dish = lax.axis_size("dish")
    total = samples * count_tm
    own_bins = PH // count_tm
    bin_count = max(own_bins, 64)
    base = lax.axis_index("tm") * own_bins
    all_bins = lax.all_gather(phase_bins, "tm", axis=0, tiled=True)
    beam = lax.psum(form_beam(voltages, beam_weights), "dish").astype(jnp.bfloat16)
    beam = lax.all_gather(beam, "tm", axis=1, tiled=True)
    beam = jnp.pad(beam.astype(jnp.float32), ((0, 0), (0, LAGS + BLOCK)))

    chunk = min(16384, total)
    steps = total // chunk
    here = chunk // BLOCK
    inside = (all_bins >= base) & (all_bins < base + own_bins)
    touched = jnp.any(inside.reshape(steps, here, BLOCK), axis=2)
    number = jnp.arange(here, dtype=jnp.int32)
    before = jnp.sum(touched[:, None, :] & (number[None, None, :] < number[None, :, None]), 2, dtype=jnp.int32)
    counts = jnp.sum(touched, 1, dtype=jnp.int32)
    hit = touched[:, None, :] & (before[:, None, :] == number[None, :, None])
    listed = jnp.sum(jnp.where(hit, number[None, None, :], 0), 2, dtype=jnp.int32)

    folded = pl.pallas_call(
        functools.partial(fold_kernel, chunk, bin_count),
        grid=(steps,),
        out_shape=jax.ShapeDtypeStruct((LAGS, 2 * bin_count), jnp.float32),
        in_specs=[pl.BlockSpec(memory_space=pltpu.SMEM)] * 3 + [pl.BlockSpec(memory_space=pltpu.VMEM)] * 2,
        out_specs=pl.BlockSpec((LAGS, 2 * bin_count), lambda step: (0, 0)),
        scratch_shapes=[
            pltpu.VMEM((2, GROUP, chunk + LAGS), jnp.float32),
            pltpu.VMEM((chunk + LAGS - BLOCK, 2 * BLOCK), jnp.bfloat16),
        ],
        compiler_params=pltpu.CompilerParams(vmem_limit_bytes=48 * 2**20),
    )(listed.reshape(-1), counts, base.reshape(1), beam, all_bins.reshape(1, total))

    real = folded[:, :own_bins]
    imag = folded[:, bin_count : bin_count + own_bins]
    turn = (lax.axis_index("dish") * jnp.arange(LAGS, dtype=jnp.int32) % count_dish).astype(jnp.float32)
    angle = turn * (2.0 * math.pi / count_dish)
    cosine, sine = jnp.cos(angle)[:, None], jnp.sin(angle)[:, None]
    coeffs = jnp.concatenate([real * cosine + imag * sine, imag * cosine - real * sine], 1)
    high = lax.reduce_precision(coeffs, 8, 7)
    split = jnp.concatenate([high, coeffs - high], 1).astype(jnp.bfloat16)
    product = jnp.dot(table, split, preferred_element_type=jnp.float32)
    product = product[:, : 2 * own_bins] + product[:, 2 * own_bins :]
    rows = LAGS // count_dish
    by_cosine, by_sine = product[:rows], product[rows:]
    scale = 1.0 / math.sqrt(LAGS * total / PH)
    out_real = by_cosine[:, :own_bins] + by_sine[:, own_bins:]
    out_imag = by_cosine[:, own_bins:] - by_sine[:, :own_bins]
    return jnp.stack([out_real, out_imag], 1) * scale


def solution(mesh):
    table = transform_table(LAGS // mesh.shape["dish"])

    def run(voltages, beam_weights, phase_bins):
        return jax.shard_map(
            functools.partial(per_device, jnp.asarray(table)),
            mesh=mesh,
            in_specs=(P(None, "dish", "tm"), P(None, "dish"), P("tm")),
            out_specs=P("dish", None, "tm"),
            check_vma=False,
        )(voltages, beam_weights, phase_bins)

    return run
```

```python
import functools
import math

import jax
import jax.numpy as jnp
import ml_dtypes
import numpy as np
from jax import lax
from jax.experimental import pallas as pl
from jax.experimental.pallas import tpu as pltpu
from jax.sharding import PartitionSpec as P

PH = 1024
LAGS = 2048
BLOCK = 128
GROUP = 16
LAG_PIECE = 512
SPAN = 1024
DIGIT = 32
UNROLL = 4


def form_beam(volt_block, weights):
    dish_count = volt_block.shape[1]
    mixer_rows = jnp.stack(
        [jnp.concatenate([weights[0], -weights[1]]), jnp.concatenate([weights[1], weights[0]])]
    )
    flat_volts = volt_block.reshape(2 * dish_count, volt_block.shape[2])
    return jnp.dot(mixer_rows, flat_volts, preferred_element_type=jnp.float32)


def fold_kernel(chunk, bin_count, list_ref, count_ref, base_ref, beam_ref, bins_ref, out_ref, shifted, hankel):
    step = pl.program_id(0)
    start = pl.multiple_of(step * chunk, BLOCK)
    width = chunk + LAGS
    blocks_here = chunk // BLOCK

    @pl.when(step == 0)
    def _():
        out_ref[...] = jnp.zeros_like(out_ref)

    count = count_ref[step]

    @pl.when(count > 0)
    def _():
        row = lax.broadcasted_iota(jnp.int32, (GROUP, SPAN + BLOCK), 0)

        def shift_rows(position, carry):
            lane = pl.multiple_of(position * SPAN, SPAN)
            for part in range(2):
                rows = jnp.broadcast_to(
                    beam_ref[pl.ds(part, 1), pl.ds(pl.multiple_of(start + lane, BLOCK), SPAN + BLOCK)],
                    (GROUP, SPAN + BLOCK),
                )
                amount = 1
                while amount < GROUP:
                    rows = jnp.where(
                        (row & amount) != 0, pltpu.roll(rows, SPAN + BLOCK - amount, 1), rows
                    )
                    amount *= 2
                shifted[part, :, pl.ds(lane, SPAN)] = rows[:, :SPAN]
            return carry

        lax.fori_loop(0, width // SPAN, shift_rows, 0)
        lane_index = lax.broadcasted_iota(jnp.int32, (GROUP, BLOCK), 1)

        def build(position, carry):
            lane = pl.multiple_of(position * UNROLL * BLOCK, UNROLL * BLOCK)
            for part in range(2):
                tiles = [
                    shifted[part, :, pl.ds(lane + tile * BLOCK, BLOCK)] for tile in range(UNROLL + 1)
                ]
                for group in range(BLOCK // GROUP):
                    offset = group * GROUP
                    for tile in range(UNROLL):
                        piece = tiles[tile]
                        if offset > 0:
                            mixed = jnp.where(lane_index < offset, tiles[tile + 1], piece)
                            piece = pltpu.roll(mixed, BLOCK - offset, 1)
                        first = pl.multiple_of(lane + tile * BLOCK + offset, GROUP)
                        hankel[pl.ds(first, GROUP), pl.ds(part * BLOCK, BLOCK)] = piece.astype(jnp.bfloat16)
            return carry

        lax.fori_loop(0, width // (UNROLL * BLOCK), build, 0)
        target = base_ref[0] + lax.broadcasted_iota(jnp.int32, (bin_count, BLOCK), 0)

        def fold(position, carry):
            row_start = pl.multiple_of(list_ref[step * blocks_here + position] * BLOCK, BLOCK)
            lane = pl.ds(pl.multiple_of(start + row_start, BLOCK), BLOCK)
            real = beam_ref[0:1, lane]
            imag = beam_ref[1:2, lane]
            chosen = bins_ref[0:1, lane] == target
            zero = jnp.zeros((bin_count, BLOCK), jnp.float32)
            chosen_real = jnp.where(chosen, real, zero)
            chosen_imag = jnp.where(chosen, imag, zero)
            right = jnp.concatenate(
                [
                    jnp.concatenate([chosen_real, chosen_imag], 1),
                    jnp.concatenate([-chosen_imag, chosen_real], 1),
                ],
                0,
            ).astype(jnp.bfloat16)
            for piece in range(LAGS // LAG_PIECE):
                rows = pl.ds(piece * LAG_PIECE, LAG_PIECE)
                left = hankel[pl.ds(pl.multiple_of(row_start + piece * LAG_PIECE, BLOCK), LAG_PIECE), :]
                out_ref[rows, :] += lax.dot_general(
                    left, right, (((1,), (1,)), ((), ())), preferred_element_type=jnp.float32
                )
            return carry

        lax.fori_loop(0, count, fold, 0)


def transform_table(row_count):
    turn = np.arange(row_count)[:, None] * np.arange(LAGS)[None, :] % LAGS
    angle = turn * (2.0 * math.pi / LAGS)
    return np.concatenate([np.cos(angle), np.sin(angle)], 0).astype(ml_dtypes.bfloat16)


def per_device(table, voltages, beam_weights, phase_bins):
    samples = phase_bins.shape[0]
    count_tm = lax.axis_size("tm")
    count_dish = lax.axis_size("dish")
    total = samples * count_tm
    own_bins = PH // count_tm
    bin_count = max(own_bins, 64)
    base = lax.axis_index("tm") * own_bins
    digits = jnp.stack([phase_bins // DIGIT, phase_bins % DIGIT]).astype(jnp.bfloat16)
    beam = lax.psum(form_beam(voltages, beam_weights), "dish").astype(jnp.bfloat16)
    gathered = lax.all_gather(jnp.concatenate([beam, digits], 0), "tm", axis=1, tiled=True)
    gathered = gathered.astype(jnp.float32)
    beam = jnp.pad(gathered[:2], ((0, 0), (0, LAGS + BLOCK)))
    all_bins = (gathered[2] * DIGIT + gathered[3]).astype(jnp.int32)

    chunk = min(32768, total)
    steps = total // chunk
    here = chunk // BLOCK
    inside = (all_bins >= base) & (all_bins < base + own_bins)
    touched = jnp.any(inside.reshape(steps, here, BLOCK), axis=2)
    number = jnp.arange(here, dtype=jnp.int32)
    before = jnp.sum(touched[:, None, :] & (number[None, None, :] < number[None, :, None]), 2, dtype=jnp.int32)
    counts = jnp.sum(touched, 1, dtype=jnp.int32)
    hit = touched[:, None, :] & (before[:, None, :] == number[None, :, None])
    listed = jnp.sum(jnp.where(hit, number[None, None, :], 0), 2, dtype=jnp.int32)

    folded = pl.pallas_call(
        functools.partial(fold_kernel, chunk, bin_count),
        grid=(steps,),
        out_shape=jax.ShapeDtypeStruct((LAGS, 2 * bin_count), jnp.float32),
        in_specs=[pl.BlockSpec(memory_space=pltpu.SMEM)] * 3 + [pl.BlockSpec(memory_space=pltpu.VMEM)] * 2,
        out_specs=pl.BlockSpec((LAGS, 2 * bin_count), lambda step: (0, 0)),
        scratch_shapes=[
            pltpu.VMEM((2, GROUP, chunk + LAGS + BLOCK), jnp.float32),
            pltpu.VMEM((chunk + LAGS, 2 * BLOCK), jnp.bfloat16),
        ],
        compiler_params=pltpu.CompilerParams(vmem_limit_bytes=48 * 2**20),
    )(listed.reshape(-1), counts, base.reshape(1), beam, all_bins.reshape(1, total))

    real = folded[:, :own_bins]
    imag = folded[:, bin_count : bin_count + own_bins]
    turn = (lax.axis_index("dish") * jnp.arange(LAGS, dtype=jnp.int32) % count_dish).astype(jnp.float32)
    angle = turn * (2.0 * math.pi / count_dish)
    cosine, sine = jnp.cos(angle)[:, None], jnp.sin(angle)[:, None]
    coeffs = jnp.concatenate([real * cosine + imag * sine, imag * cosine - real * sine], 1)
    high = lax.reduce_precision(coeffs, 8, 7)
    split = jnp.concatenate([high, coeffs - high], 1).astype(jnp.bfloat16)
    product = jnp.dot(table, split, preferred_element_type=jnp.float32)
    product = product[:, : 2 * own_bins] + product[:, 2 * own_bins :]
    rows = LAGS // count_dish
    by_cosine, by_sine = product[:rows], product[rows:]
    scale = 1.0 / math.sqrt(LAGS * total / PH)
    out_real = by_cosine[:, :own_bins] + by_sine[:, own_bins:]
    out_imag = by_cosine[:, own_bins:] - by_sine[:, :own_bins]
    return jnp.stack([out_real, out_imag], 1) * scale


def solution(mesh):
    table = transform_table(LAGS // mesh.shape["dish"])

    def run(voltages, beam_weights, phase_bins):
        return jax.shard_map(
            functools.partial(per_device, jnp.asarray(table)),
            mesh=mesh,
            in_specs=(P(None, "dish", "tm"), P(None, "dish"), P("tm")),
            out_specs=P("dish", None, "tm"),
            check_vma=False,
        )(voltages, beam_weights, phase_bins)

    return run
```

```python
import functools
import math

import jax
import jax.numpy as jnp
import ml_dtypes
import numpy as np
from jax import lax
from jax.experimental import pallas as pl
from jax.experimental.pallas import tpu as pltpu
from jax.sharding import PartitionSpec as P

PH = 1024
LAGS = 2048
BLOCK = 128
GROUP = 16
LAG_PIECE = 512
SPAN = 1024
DIGIT = 32
UNROLL = 4


def form_beam(volt_block, weights):
    dish_count = volt_block.shape[1]
    mixer_rows = jnp.stack(
        [jnp.concatenate([weights[0], -weights[1]]), jnp.concatenate([weights[1], weights[0]])]
    )
    flat_volts = volt_block.reshape(2 * dish_count, volt_block.shape[2])
    return jnp.dot(mixer_rows, flat_volts, preferred_element_type=jnp.float32)


def fold_kernel(chunk, bin_count, list_ref, count_ref, base_ref, beam_ref, bins_ref, out_ref, shifted, hankel, total):
    step = pl.program_id(0)
    start = pl.multiple_of(step * chunk, BLOCK)
    width = chunk + LAGS
    blocks_here = chunk // BLOCK

    @pl.when(step == 0)
    def _():
        total[...] = jnp.zeros_like(total)
        shifted[:, :, width:] = jnp.zeros((2, GROUP, BLOCK), jnp.float32)

    count = count_ref[step]

    @pl.when(count > 0)
    def _():
        row = lax.broadcasted_iota(jnp.int32, (GROUP, SPAN + BLOCK), 0)

        def shift_rows(position, carry):
            lane = pl.multiple_of(position * SPAN, SPAN)
            for part in range(2):
                rows = jnp.broadcast_to(
                    beam_ref[pl.ds(part, 1), pl.ds(pl.multiple_of(start + lane, BLOCK), SPAN + BLOCK)],
                    (GROUP, SPAN + BLOCK),
                )
                amount = 1
                while amount < GROUP:
                    rows = jnp.where(
                        (row & amount) != 0, pltpu.roll(rows, SPAN + BLOCK - amount, 1), rows
                    )
                    amount *= 2
                shifted[part, :, pl.ds(lane, SPAN)] = rows[:, :SPAN]
            return carry

        lax.fori_loop(0, width // SPAN, shift_rows, 0)
        lane_index = lax.broadcasted_iota(jnp.int32, (GROUP, BLOCK), 1)

        def build(position, carry):
            lane = pl.multiple_of(position * UNROLL * BLOCK, UNROLL * BLOCK)
            for part in range(2):
                tiles = [
                    shifted[part, :, pl.ds(lane + tile * BLOCK, BLOCK)] for tile in range(UNROLL + 1)
                ]
                for group in range(BLOCK // GROUP):
                    offset = group * GROUP
                    for tile in range(UNROLL):
                        piece = tiles[tile]
                        if offset > 0:
                            mixed = jnp.where(lane_index < offset, tiles[tile + 1], piece)
                            piece = pltpu.roll(mixed, BLOCK - offset, 1)
                        first = pl.multiple_of(lane + tile * BLOCK + offset, GROUP)
                        hankel[pl.ds(first, GROUP), pl.ds(part * BLOCK, BLOCK)] = piece.astype(jnp.bfloat16)
            return carry

        lax.fori_loop(0, width // (UNROLL * BLOCK), build, 0)
        target = base_ref[0] + lax.broadcasted_iota(jnp.int32, (bin_count, BLOCK), 0)

        def chosen_rows(lane, wanted):
            real = beam_ref[0:1, lane]
            imag = beam_ref[1:2, lane]
            chosen = bins_ref[0:1, lane] == wanted
            zero = jnp.zeros((bin_count, BLOCK), jnp.float32)
            chosen_real = jnp.where(chosen, real, zero)
            chosen_imag = jnp.where(chosen, imag, zero)
            return [
                jnp.concatenate([chosen_real, chosen_imag], 1),
                jnp.concatenate([-chosen_imag, chosen_real], 1),
            ]

        def fold(position, carry):
            block = list_ref[step * blocks_here + position]
            row_start = pl.multiple_of(block * BLOCK, BLOCK)
            lane = pl.multiple_of(start + row_start, BLOCK)
            inside = block + 1 < blocks_here
            after = pl.multiple_of(jnp.where(inside, lane + BLOCK, lane), BLOCK)
            right = jnp.concatenate(
                chosen_rows(pl.ds(lane, BLOCK), target)
                + chosen_rows(pl.ds(after, BLOCK), jnp.where(inside, target, -1)),
                0,
            ).astype(jnp.bfloat16)
            first = 0
            while first < LAGS + BLOCK:
                size = min(LAG_PIECE, LAGS + BLOCK - first)
                left = hankel[pl.ds(pl.multiple_of(row_start + first, BLOCK), size), :]
                total[pl.ds(first, size), :] += lax.dot_general(
                    left, right, (((1,), (1,)), ((), ())), preferred_element_type=jnp.float32
                )
                first += size
            return carry

        lax.fori_loop(0, count, fold, 0)

    @pl.when(step == pl.num_programs(0) - 1)
    def _():
        out_ref[...] = total[:LAGS, : 2 * bin_count] + total[BLOCK:, 2 * bin_count :]


def transform_table(row_count):
    turn = np.arange(row_count)[:, None] * np.arange(LAGS)[None, :] % LAGS
    angle = turn * (2.0 * math.pi / LAGS)
    return np.concatenate([np.cos(angle), np.sin(angle)], 0).astype(ml_dtypes.bfloat16)


def per_device(table, voltages, beam_weights, phase_bins):
    samples = phase_bins.shape[0]
    count_tm = lax.axis_size("tm")
    count_dish = lax.axis_size("dish")
    total = samples * count_tm
    own_bins = PH // count_tm
    bin_count = max(own_bins, 64)
    base = lax.axis_index("tm") * own_bins
    digits = jnp.stack([phase_bins // DIGIT, phase_bins % DIGIT]).astype(jnp.bfloat16)
    beam = lax.psum(form_beam(voltages, beam_weights), "dish").astype(jnp.bfloat16)
    gathered = lax.all_gather(jnp.concatenate([beam, digits], 0), "tm", axis=1, tiled=True)
    gathered = gathered.astype(jnp.float32)
    beam = jnp.pad(gathered[:2], ((0, 0), (0, LAGS + BLOCK)))
    all_bins = (gathered[2] * DIGIT + gathered[3]).astype(jnp.int32)

    chunk = min(32768, total)
    steps = total // chunk
    here = chunk // BLOCK
    inside = (all_bins >= base) & (all_bins < base + own_bins)
    touched = jnp.any(inside.reshape(steps, here, BLOCK), axis=2)
    number = jnp.arange(here, dtype=jnp.int32)
    gap = ~touched[:, None, :] & (number[None, None, :] < number[None, :, None])
    last_gap = jnp.max(jnp.where(gap, number[None, None, :], -1), 2)
    touched = touched & ((number[None, :] - last_gap) % 2 == 1)
    before = jnp.sum(touched[:, None, :] & (number[None, None, :] < number[None, :, None]), 2, dtype=jnp.int32)
    counts = jnp.sum(touched, 1, dtype=jnp.int32)
    hit = touched[:, None, :] & (before[:, None, :] == number[None, :, None])
    listed = jnp.sum(jnp.where(hit, number[None, None, :], 0), 2, dtype=jnp.int32)

    folded = pl.pallas_call(
        functools.partial(fold_kernel, chunk, bin_count),
        grid=(steps,),
        out_shape=jax.ShapeDtypeStruct((LAGS, 2 * bin_count), jnp.float32),
        in_specs=[pl.BlockSpec(memory_space=pltpu.SMEM)] * 3 + [pl.BlockSpec(memory_space=pltpu.VMEM)] * 2,
        out_specs=pl.BlockSpec((LAGS, 2 * bin_count), lambda step: (0, 0)),
        scratch_shapes=[
            pltpu.VMEM((2, GROUP, chunk + LAGS + BLOCK), jnp.float32),
            pltpu.VMEM((chunk + LAGS, 2 * BLOCK), jnp.bfloat16),
            pltpu.VMEM((LAGS + BLOCK, 4 * bin_count), jnp.float32),
        ],
        compiler_params=pltpu.CompilerParams(vmem_limit_bytes=48 * 2**20),
    )(listed.reshape(-1), counts, base.reshape(1), beam, all_bins.reshape(1, total))

    real = folded[:, :own_bins]
    imag = folded[:, bin_count : bin_count + own_bins]
    turn = (lax.axis_index("dish") * jnp.arange(LAGS, dtype=jnp.int32) % count_dish).astype(jnp.float32)
    angle = turn * (2.0 * math.pi / count_dish)
    cosine, sine = jnp.cos(angle)[:, None], jnp.sin(angle)[:, None]
    coeffs = jnp.concatenate([real * cosine + imag * sine, imag * cosine - real * sine], 1)
    high = lax.reduce_precision(coeffs, 8, 7)
    split = jnp.concatenate([high, coeffs - high], 1).astype(jnp.bfloat16)
    product = jnp.dot(table, split, preferred_element_type=jnp.float32)
    product = product[:, : 2 * own_bins] + product[:, 2 * own_bins :]
    rows = LAGS // count_dish
    by_cosine, by_sine = product[:rows], product[rows:]
    scale = 1.0 / math.sqrt(LAGS * total / PH)
    out_real = by_cosine[:, :own_bins] + by_sine[:, own_bins:]
    out_imag = by_cosine[:, own_bins:] - by_sine[:, :own_bins]
    return jnp.stack([out_real, out_imag], 1) * scale


def solution(mesh):
    table = transform_table(LAGS // mesh.shape["dish"])

    def run(voltages, beam_weights, phase_bins):
        return jax.shard_map(
            functools.partial(per_device, jnp.asarray(table)),
            mesh=mesh,
            in_specs=(P(None, "dish", "tm"), P(None, "dish"), P("tm")),
            out_specs=P("dish", None, "tm"),
            check_vma=False,
        )(voltages, beam_weights, phase_bins)

    return run
```

```python
import functools
import math

import jax
import jax.numpy as jnp
import ml_dtypes
import numpy as np
from jax import lax
from jax.experimental import pallas as pl
from jax.experimental.pallas import tpu as pltpu
from jax.sharding import PartitionSpec as P

PH = 1024
LAGS = 2048
BLOCK = 128
GROUP = 16
LAG_PIECE = 512
SPAN = 1024
DIGIT = 32
UNROLL = 4


def form_beam(volt_block, weights):
    dish_count = volt_block.shape[1]
    mixer_rows = jnp.stack(
        [jnp.concatenate([weights[0], -weights[1]]), jnp.concatenate([weights[1], weights[0]])]
    )
    flat_volts = volt_block.reshape(2 * dish_count, volt_block.shape[2])
    return jnp.dot(mixer_rows, flat_volts, preferred_element_type=jnp.float32)


def gather_kernel(count_tm, count_dish, part_ref, digit_ref, out_ref, arrived, sem_part, sem_block):
    me = lax.axis_index("tm")
    mine = lax.axis_index("dish")
    barrier = pltpu.get_barrier_semaphore()
    for away in range(1, count_tm):
        pl.semaphore_signal(
            barrier, inc=1, device_id={"tm": lax.rem(me + away, count_tm)}, device_id_type=pl.DeviceIdType.MESH
        )
    for away in range(1, count_dish):
        pl.semaphore_signal(
            barrier, inc=1, device_id={"dish": lax.rem(mine + away, count_dish)}, device_id_type=pl.DeviceIdType.MESH
        )
    pl.semaphore_wait(barrier, count_tm + count_dish - 2)
    copies = []
    for away in range(1, count_dish):
        copy = pltpu.make_async_remote_copy(
            src_ref=part_ref,
            dst_ref=arrived.at[away - 1],
            send_sem=sem_part.at[0, away - 1],
            recv_sem=sem_part.at[1, away - 1],
            device_id={"dish": lax.rem(mine + away, count_dish)},
            device_id_type=pl.DeviceIdType.MESH,
        )
        copy.start()
        copies.append(copy)
    rows = part_ref.shape[0]
    out_ref[me, rows:, :] = digit_ref[...]
    beam = part_ref[...]
    for away, copy in enumerate(copies):
        copy.wait()
        beam = beam + arrived[away]
    out_ref[me, :rows, :] = beam.astype(jnp.bfloat16)
    copies = []
    for away in range(1, count_tm):
        copy = pltpu.make_async_remote_copy(
            src_ref=out_ref.at[me],
            dst_ref=out_ref.at[me],
            send_sem=sem_block.at[0, away - 1],
            recv_sem=sem_block.at[1, away - 1],
            device_id={"tm": lax.rem(me + away, count_tm)},
            device_id_type=pl.DeviceIdType.MESH,
        )
        copy.start()
        copies.append(copy)
    for copy in copies:
        copy.wait()


def gather_beam(partial, digits, count_tm, count_dish):
    rows = partial.size // BLOCK
    blocks = pl.pallas_call(
        functools.partial(gather_kernel, count_tm, count_dish),
        out_shape=jax.ShapeDtypeStruct((count_tm, 2 * rows, BLOCK), jnp.bfloat16),
        in_specs=[pl.BlockSpec(memory_space=pltpu.VMEM)] * 2,
        out_specs=pl.BlockSpec(memory_space=pltpu.VMEM),
        scratch_shapes=[
            pltpu.VMEM((max(1, count_dish - 1), rows, BLOCK), jnp.float32),
            pltpu.SemaphoreType.DMA((2, max(1, count_dish - 1))),
            pltpu.SemaphoreType.DMA((2, max(1, count_tm - 1))),
        ],
        compiler_params=pltpu.CompilerParams(
            collective_id=0, has_side_effects=True, vmem_limit_bytes=16 * 2**20
        ),
    )(partial.reshape(rows, BLOCK), digits.reshape(rows, BLOCK))
    samples = partial.shape[1]
    return jnp.swapaxes(blocks.reshape(count_tm, 4, samples), 0, 1).reshape(4, count_tm * samples)


def fold_kernel(chunk, bin_count, list_ref, count_ref, base_ref, beam_ref, bins_ref, out_ref, shifted, hankel, total):
    step = pl.program_id(0)
    start = pl.multiple_of(step * chunk, BLOCK)
    width = chunk + LAGS
    blocks_here = chunk // BLOCK

    @pl.when(step == 0)
    def _():
        total[...] = jnp.zeros_like(total)
        shifted[:, :, width:] = jnp.zeros((2, GROUP, BLOCK), jnp.float32)

    count = count_ref[step]

    @pl.when(count > 0)
    def _():
        row = lax.broadcasted_iota(jnp.int32, (GROUP, SPAN + BLOCK), 0)

        def shift_rows(position, carry):
            lane = pl.multiple_of(position * SPAN, SPAN)
            for part in range(2):
                rows = jnp.broadcast_to(
                    beam_ref[pl.ds(part, 1), pl.ds(pl.multiple_of(start + lane, BLOCK), SPAN + BLOCK)],
                    (GROUP, SPAN + BLOCK),
                )
                amount = 1
                while amount < GROUP:
                    rows = jnp.where(
                        (row & amount) != 0, pltpu.roll(rows, SPAN + BLOCK - amount, 1), rows
                    )
                    amount *= 2
                shifted[part, :, pl.ds(lane, SPAN)] = rows[:, :SPAN]
            return carry

        lax.fori_loop(0, width // SPAN, shift_rows, 0)
        lane_index = lax.broadcasted_iota(jnp.int32, (GROUP, BLOCK), 1)

        def build(position, carry):
            lane = pl.multiple_of(position * UNROLL * BLOCK, UNROLL * BLOCK)
            for part in range(2):
                tiles = [
                    shifted[part, :, pl.ds(lane + tile * BLOCK, BLOCK)] for tile in range(UNROLL + 1)
                ]
                for group in range(BLOCK // GROUP):
                    offset = group * GROUP
                    for tile in range(UNROLL):
                        piece = tiles[tile]
                        if offset > 0:
                            mixed = jnp.where(lane_index < offset, tiles[tile + 1], piece)
                            piece = pltpu.roll(mixed, BLOCK - offset, 1)
                        first = pl.multiple_of(lane + tile * BLOCK + offset, GROUP)
                        hankel[pl.ds(first, GROUP), pl.ds(part * BLOCK, BLOCK)] = piece.astype(jnp.bfloat16)
            return carry

        lax.fori_loop(0, width // (UNROLL * BLOCK), build, 0)
        target = base_ref[0] + lax.broadcasted_iota(jnp.int32, (bin_count, BLOCK), 0)

        def chosen_rows(lane, wanted):
            real = beam_ref[0:1, lane]
            imag = beam_ref[1:2, lane]
            chosen = bins_ref[0:1, lane] == wanted
            zero = jnp.zeros((bin_count, BLOCK), jnp.float32)
            chosen_real = jnp.where(chosen, real, zero)
            chosen_imag = jnp.where(chosen, imag, zero)
            return [
                jnp.concatenate([chosen_real, chosen_imag], 1),
                jnp.concatenate([-chosen_imag, chosen_real], 1),
            ]

        def fold(position, carry):
            block = list_ref[step * blocks_here + position]
            row_start = pl.multiple_of(block * BLOCK, BLOCK)
            lane = pl.multiple_of(start + row_start, BLOCK)
            inside = block + 1 < blocks_here
            after = pl.multiple_of(jnp.where(inside, lane + BLOCK, lane), BLOCK)
            right = jnp.concatenate(
                chosen_rows(pl.ds(lane, BLOCK), target)
                + chosen_rows(pl.ds(after, BLOCK), jnp.where(inside, target, -1)),
                0,
            ).astype(jnp.bfloat16)
            first = 0
            while first < LAGS + BLOCK:
                size = min(LAG_PIECE, LAGS + BLOCK - first)
                left = hankel[pl.ds(pl.multiple_of(row_start + first, BLOCK), size), :]
                total[pl.ds(first, size), :] += lax.dot_general(
                    left, right, (((1,), (1,)), ((), ())), preferred_element_type=jnp.float32
                )
                first += size
            return carry

        lax.fori_loop(0, count, fold, 0)

    @pl.when(step == pl.num_programs(0) - 1)
    def _():
        out_ref[...] = total[:LAGS, : 2 * bin_count] + total[BLOCK:, 2 * bin_count :]


def transform_table(row_count):
    turn = np.arange(row_count)[:, None] * np.arange(LAGS)[None, :] % LAGS
    angle = turn * (2.0 * math.pi / LAGS)
    return np.concatenate([np.cos(angle), np.sin(angle)], 0).astype(ml_dtypes.bfloat16)


def per_device(table, voltages, beam_weights, phase_bins):
    samples = phase_bins.shape[0]
    count_tm = lax.axis_size("tm")
    count_dish = lax.axis_size("dish")
    total = samples * count_tm
    own_bins = PH // count_tm
    bin_count = max(own_bins, 64)
    base = lax.axis_index("tm") * own_bins
    digits = jnp.stack([phase_bins // DIGIT, phase_bins % DIGIT]).astype(jnp.bfloat16)
    gathered = gather_beam(form_beam(voltages, beam_weights), digits, count_tm, count_dish)
    gathered = gathered.astype(jnp.float32)
    beam = jnp.pad(gathered[:2], ((0, 0), (0, LAGS + BLOCK)))
    all_bins = (gathered[2] * DIGIT + gathered[3]).astype(jnp.int32)

    chunk = min(32768, total)
    steps = total // chunk
    here = chunk // BLOCK
    inside = (all_bins >= base) & (all_bins < base + own_bins)
    touched = jnp.any(inside.reshape(steps, here, BLOCK), axis=2)
    number = jnp.arange(here, dtype=jnp.int32)
    gap = ~touched[:, None, :] & (number[None, None, :] < number[None, :, None])
    last_gap = jnp.max(jnp.where(gap, number[None, None, :], -1), 2)
    touched = touched & ((number[None, :] - last_gap) % 2 == 1)
    before = jnp.sum(touched[:, None, :] & (number[None, None, :] < number[None, :, None]), 2, dtype=jnp.int32)
    counts = jnp.sum(touched, 1, dtype=jnp.int32)
    hit = touched[:, None, :] & (before[:, None, :] == number[None, :, None])
    listed = jnp.sum(jnp.where(hit, number[None, None, :], 0), 2, dtype=jnp.int32)

    folded = pl.pallas_call(
        functools.partial(fold_kernel, chunk, bin_count),
        grid=(steps,),
        out_shape=jax.ShapeDtypeStruct((LAGS, 2 * bin_count), jnp.float32),
        in_specs=[pl.BlockSpec(memory_space=pltpu.SMEM)] * 3 + [pl.BlockSpec(memory_space=pltpu.VMEM)] * 2,
        out_specs=pl.BlockSpec((LAGS, 2 * bin_count), lambda step: (0, 0)),
        scratch_shapes=[
            pltpu.VMEM((2, GROUP, chunk + LAGS + BLOCK), jnp.float32),
            pltpu.VMEM((chunk + LAGS, 2 * BLOCK), jnp.bfloat16),
            pltpu.VMEM((LAGS + BLOCK, 4 * bin_count), jnp.float32),
        ],
        compiler_params=pltpu.CompilerParams(vmem_limit_bytes=48 * 2**20),
    )(listed.reshape(-1), counts, base.reshape(1), beam, all_bins.reshape(1, total))

    real = folded[:, :own_bins]
    imag = folded[:, bin_count : bin_count + own_bins]
    turn = (lax.axis_index("dish") * jnp.arange(LAGS, dtype=jnp.int32) % count_dish).astype(jnp.float32)
    angle = turn * (2.0 * math.pi / count_dish)
    cosine, sine = jnp.cos(angle)[:, None], jnp.sin(angle)[:, None]
    coeffs = jnp.concatenate([real * cosine + imag * sine, imag * cosine - real * sine], 1)
    high = lax.reduce_precision(coeffs, 8, 7)
    split = jnp.concatenate([high, coeffs - high], 1).astype(jnp.bfloat16)
    product = jnp.dot(table, split, preferred_element_type=jnp.float32)
    product = product[:, : 2 * own_bins] + product[:, 2 * own_bins :]
    rows = LAGS // count_dish
    by_cosine, by_sine = product[:rows], product[rows:]
    scale = 1.0 / math.sqrt(LAGS * total / PH)
    out_real = by_cosine[:, :own_bins] + by_sine[:, own_bins:]
    out_imag = by_cosine[:, own_bins:] - by_sine[:, :own_bins]
    return jnp.stack([out_real, out_imag], 1) * scale


def solution(mesh):
    table = transform_table(LAGS // mesh.shape["dish"])

    def run(voltages, beam_weights, phase_bins):
        return jax.shard_map(
            functools.partial(per_device, jnp.asarray(table)),
            mesh=mesh,
            in_specs=(P(None, "dish", "tm"), P(None, "dish"), P("tm")),
            out_specs=P("dish", None, "tm"),
            check_vma=False,
        )(voltages, beam_weights, phase_bins)

    return run
```

```python
import functools
import math

import jax
import jax.numpy as jnp
import ml_dtypes
import numpy as np
from jax import lax
from jax.experimental import pallas as pl
from jax.experimental.pallas import tpu as pltpu
from jax.sharding import PartitionSpec as P

PH = 1024
LAGS = 2048
BLOCK = 128
GROUP = 16
LAG_PIECE = 512
SPAN = 1024
DIGIT = 32
UNROLL = 4


def form_beam(volt_block, weights):
    dish_count = volt_block.shape[1]
    mixer_rows = jnp.stack(
        [jnp.concatenate([weights[0], -weights[1]]), jnp.concatenate([weights[1], weights[0]])]
    )
    flat_volts = volt_block.reshape(2 * dish_count, volt_block.shape[2])
    return jnp.dot(mixer_rows, flat_volts, preferred_element_type=jnp.float32)


def gather_kernel(count_tm, count_dish, part_ref, digit_ref, out_ref, arrived, sem_part, sem_block):
    me = lax.axis_index("tm")
    mine = lax.axis_index("dish")
    barrier = pltpu.get_barrier_semaphore()
    for away in range(1, count_tm):
        pl.semaphore_signal(
            barrier, inc=1, device_id={"tm": lax.rem(me + away, count_tm)}, device_id_type=pl.DeviceIdType.MESH
        )
    for away in range(1, count_dish):
        pl.semaphore_signal(
            barrier, inc=1, device_id={"dish": lax.rem(mine + away, count_dish)}, device_id_type=pl.DeviceIdType.MESH
        )
    pl.semaphore_wait(barrier, count_tm + count_dish - 2)
    copies = []
    for away in range(1, count_dish):
        copy = pltpu.make_async_remote_copy(
            src_ref=part_ref,
            dst_ref=arrived.at[away - 1],
            send_sem=sem_part.at[0, away - 1],
            recv_sem=sem_part.at[1, away - 1],
            device_id={"dish": lax.rem(mine + away, count_dish)},
            device_id_type=pl.DeviceIdType.MESH,
        )
        copy.start()
        copies.append(copy)
    rows = part_ref.shape[0]
    out_ref[me, rows:, :] = digit_ref[...]
    beam = part_ref[...]
    for away, copy in enumerate(copies):
        copy.wait()
        beam = beam + arrived[away]
    out_ref[me, :rows, :] = beam.astype(jnp.bfloat16)
    copies = []
    for away in range(1, count_tm):
        copy = pltpu.make_async_remote_copy(
            src_ref=out_ref.at[me],
            dst_ref=out_ref.at[me],
            send_sem=sem_block.at[0, away - 1],
            recv_sem=sem_block.at[1, away - 1],
            device_id={"tm": lax.rem(me + away, count_tm)},
            device_id_type=pl.DeviceIdType.MESH,
        )
        copy.start()
        copies.append(copy)
    for copy in copies:
        copy.wait()


def gather_beam(partial, digits, count_tm, count_dish):
    rows = partial.size // BLOCK
    blocks = pl.pallas_call(
        functools.partial(gather_kernel, count_tm, count_dish),
        out_shape=jax.ShapeDtypeStruct((count_tm, 2 * rows, BLOCK), jnp.bfloat16),
        in_specs=[pl.BlockSpec(memory_space=pltpu.VMEM)] * 2,
        out_specs=pl.BlockSpec(memory_space=pltpu.VMEM),
        scratch_shapes=[
            pltpu.VMEM((max(1, count_dish - 1), rows, BLOCK), jnp.float32),
            pltpu.SemaphoreType.DMA((2, max(1, count_dish - 1))),
            pltpu.SemaphoreType.DMA((2, max(1, count_tm - 1))),
        ],
        compiler_params=pltpu.CompilerParams(
            collective_id=0, has_side_effects=True, vmem_limit_bytes=16 * 2**20
        ),
    )(partial.reshape(rows, BLOCK), digits.reshape(rows, BLOCK))
    samples = partial.shape[1]
    return jnp.swapaxes(blocks.reshape(count_tm, 4, samples), 0, 1).reshape(4, count_tm * samples)


def fold_kernel(chunk, bin_count, list_ref, count_ref, base_ref, beam_ref, bins_ref, out_ref, shifted, hankel, total):
    step = pl.program_id(0)
    start = pl.multiple_of(step * chunk, BLOCK)
    width = chunk + LAGS
    blocks_here = chunk // BLOCK

    @pl.when(step == 0)
    def _():
        total[...] = jnp.zeros_like(total)
        shifted[:, :, width:] = jnp.zeros((2, GROUP, BLOCK), jnp.float32)

    count = count_ref[step]

    @pl.when(count > 0)
    def _():
        half = GROUP // 2
        row = lax.broadcasted_iota(jnp.int32, (half, SPAN + BLOCK), 0)

        def shift_rows(position, carry):
            lane = pl.multiple_of(position * SPAN, SPAN)
            for part in range(2):
                rows = jnp.broadcast_to(
                    beam_ref[pl.ds(part, 1), pl.ds(pl.multiple_of(start + lane, BLOCK), SPAN + BLOCK)],
                    (half, SPAN + BLOCK),
                )
                amount = 1
                while amount < half:
                    rows = jnp.where(
                        (row & amount) != 0, pltpu.roll(rows, SPAN + BLOCK - amount, 1), rows
                    )
                    amount *= 2
                later = pltpu.roll(rows, SPAN + BLOCK - half, 1)
                shifted[part, :half, pl.ds(lane, SPAN)] = rows[:, :SPAN]
                shifted[part, half:, pl.ds(lane, SPAN)] = later[:, :SPAN]
            return carry

        lax.fori_loop(0, width // SPAN, shift_rows, 0)
        lane_index = lax.broadcasted_iota(jnp.int32, (GROUP, BLOCK), 1)

        def build(position, carry):
            lane = pl.multiple_of(position * UNROLL * BLOCK, UNROLL * BLOCK)
            for part in range(2):
                tiles = [
                    shifted[part, :, pl.ds(lane + tile * BLOCK, BLOCK)] for tile in range(UNROLL + 1)
                ]
                for group in range(BLOCK // GROUP):
                    offset = group * GROUP
                    for tile in range(UNROLL):
                        piece = tiles[tile]
                        if offset > 0:
                            mixed = jnp.where(lane_index < offset, tiles[tile + 1], piece)
                            piece = pltpu.roll(mixed, BLOCK - offset, 1)
                        first = pl.multiple_of(lane + tile * BLOCK + offset, GROUP)
                        hankel[pl.ds(first, GROUP), pl.ds(part * BLOCK, BLOCK)] = piece.astype(jnp.bfloat16)
            return carry

        lax.fori_loop(0, width // (UNROLL * BLOCK), build, 0)
        target = base_ref[0] + lax.broadcasted_iota(jnp.int32, (bin_count, BLOCK), 0)

        def chosen_rows(lane, wanted):
            real = beam_ref[0:1, lane]
            imag = beam_ref[1:2, lane]
            chosen = bins_ref[0:1, lane] == wanted
            zero = jnp.zeros((bin_count, BLOCK), jnp.float32)
            chosen_real = jnp.where(chosen, real, zero)
            chosen_imag = jnp.where(chosen, imag, zero)
            return [
                jnp.concatenate([chosen_real, chosen_imag], 1),
                jnp.concatenate([-chosen_imag, chosen_real], 1),
            ]

        def fold(position, carry):
            block = list_ref[step * blocks_here + position]
            row_start = pl.multiple_of(block * BLOCK, BLOCK)
            lane = pl.multiple_of(start + row_start, BLOCK)
            inside = block + 1 < blocks_here
            after = pl.multiple_of(jnp.where(inside, lane + BLOCK, lane), BLOCK)
            right = jnp.concatenate(
                chosen_rows(pl.ds(lane, BLOCK), target)
                + chosen_rows(pl.ds(after, BLOCK), jnp.where(inside, target, -1)),
                0,
            ).astype(jnp.bfloat16)
            first = 0
            while first < LAGS + BLOCK:
                size = min(LAG_PIECE, LAGS + BLOCK - first)
                left = hankel[pl.ds(pl.multiple_of(row_start + first, BLOCK), size), :]
                total[pl.ds(first, size), :] += lax.dot_general(
                    left, right, (((1,), (1,)), ((), ())), preferred_element_type=jnp.float32
                )
                first += size
            return carry

        lax.fori_loop(0, count, fold, 0)

    @pl.when(step == pl.num_programs(0) - 1)
    def _():
        out_ref[...] = total[:LAGS, : 2 * bin_count] + total[BLOCK:, 2 * bin_count :]


def transform_table(row_count):
    turn = np.arange(row_count)[:, None] * np.arange(LAGS)[None, :] % LAGS
    angle = turn * (2.0 * math.pi / LAGS)
    return np.concatenate([np.cos(angle), np.sin(angle)], 0).astype(ml_dtypes.bfloat16)


def per_device(table, voltages, beam_weights, phase_bins):
    samples = phase_bins.shape[0]
    count_tm = lax.axis_size("tm")
    count_dish = lax.axis_size("dish")
    total = samples * count_tm
    own_bins = PH // count_tm
    bin_count = max(own_bins, 64)
    base = lax.axis_index("tm") * own_bins
    digits = jnp.stack([phase_bins // DIGIT, phase_bins % DIGIT]).astype(jnp.bfloat16)
    gathered = gather_beam(form_beam(voltages, beam_weights), digits, count_tm, count_dish)
    gathered = gathered.astype(jnp.float32)
    beam = jnp.pad(gathered[:2], ((0, 0), (0, LAGS + BLOCK)))
    all_bins = (gathered[2] * DIGIT + gathered[3]).astype(jnp.int32)

    chunk = min(32768, total)
    steps = total // chunk
    here = chunk // BLOCK
    inside = (all_bins >= base) & (all_bins < base + own_bins)
    touched = jnp.any(inside.reshape(steps, here, BLOCK), axis=2)
    number = jnp.arange(here, dtype=jnp.int32)
    gap = ~touched[:, None, :] & (number[None, None, :] < number[None, :, None])
    last_gap = jnp.max(jnp.where(gap, number[None, None, :], -1), 2)
    touched = touched & ((number[None, :] - last_gap) % 2 == 1)
    before = jnp.sum(touched[:, None, :] & (number[None, None, :] < number[None, :, None]), 2, dtype=jnp.int32)
    counts = jnp.sum(touched, 1, dtype=jnp.int32)
    hit = touched[:, None, :] & (before[:, None, :] == number[None, :, None])
    listed = jnp.sum(jnp.where(hit, number[None, None, :], 0), 2, dtype=jnp.int32)

    folded = pl.pallas_call(
        functools.partial(fold_kernel, chunk, bin_count),
        grid=(steps,),
        out_shape=jax.ShapeDtypeStruct((LAGS, 2 * bin_count), jnp.float32),
        in_specs=[pl.BlockSpec(memory_space=pltpu.SMEM)] * 3 + [pl.BlockSpec(memory_space=pltpu.VMEM)] * 2,
        out_specs=pl.BlockSpec((LAGS, 2 * bin_count), lambda step: (0, 0)),
        scratch_shapes=[
            pltpu.VMEM((2, GROUP, chunk + LAGS + BLOCK), jnp.float32),
            pltpu.VMEM((chunk + LAGS, 2 * BLOCK), jnp.bfloat16),
            pltpu.VMEM((LAGS + BLOCK, 4 * bin_count), jnp.float32),
        ],
        compiler_params=pltpu.CompilerParams(vmem_limit_bytes=48 * 2**20),
    )(listed.reshape(-1), counts, base.reshape(1), beam, all_bins.reshape(1, total))

    real = folded[:, :own_bins]
    imag = folded[:, bin_count : bin_count + own_bins]
    turn = (lax.axis_index("dish") * jnp.arange(LAGS, dtype=jnp.int32) % count_dish).astype(jnp.float32)
    angle = turn * (2.0 * math.pi / count_dish)
    cosine, sine = jnp.cos(angle)[:, None], jnp.sin(angle)[:, None]
    coeffs = jnp.concatenate([real * cosine + imag * sine, imag * cosine - real * sine], 1)
    high = lax.reduce_precision(coeffs, 8, 7)
    split = jnp.concatenate([high, coeffs - high], 1).astype(jnp.bfloat16)
    product = jnp.dot(table, split, preferred_element_type=jnp.float32)
    product = product[:, : 2 * own_bins] + product[:, 2 * own_bins :]
    rows = LAGS // count_dish
    by_cosine, by_sine = product[:rows], product[rows:]
    scale = 1.0 / math.sqrt(LAGS * total / PH)
    out_real = by_cosine[:, :own_bins] + by_sine[:, own_bins:]
    out_imag = by_cosine[:, own_bins:] - by_sine[:, :own_bins]
    return jnp.stack([out_real, out_imag], 1) * scale


def solution(mesh):
    table = transform_table(LAGS // mesh.shape["dish"])

    def run(voltages, beam_weights, phase_bins):
        return jax.shard_map(
            functools.partial(per_device, jnp.asarray(table)),
            mesh=mesh,
            in_specs=(P(None, "dish", "tm"), P(None, "dish"), P("tm")),
            out_specs=P("dish", None, "tm"),
            check_vma=False,
        )(voltages, beam_weights, phase_bins)

    return run
```
